512 devices in a mesh: blk: 64 (over y, x, z_hi, core), layer: 8 (over z_lo).
Axes of the slice: x: 4, y: 4, z: 16 (z_hi: 2, z_lo: 8; z = z_hi * 8 + z_lo), core: 2. Of those that a mesh axis runs over, the one named last changes fastest.
Arguments:
- train_factors: bfloat16 [768, 8, 2, 64, 1024], P('blk', 'layer'), may hold values from -0.29882812 to 0.29882812
- val_factors: bfloat16 [256, 8, 2, 64, 1024], P('blk', 'layer'), may hold values from -0.29882812 to 0.29882812
Outputs:
- scores: float32 [768, 3, 4], P('blk')
The draws below stay inside these ranges and needn't reach their ends.
All inputs are finite; a program needn't handle non-finite values.
Results may differ from the reference program's by a relative error of at most 0.0003.
Values may be sent and summed in bfloat16 or wider, within the bound.
A program may use at most 64 MiB of HBM per device.

```python
import jax
import jax.numpy as jnp
from jax import lax

R = 1024
TOK = 64
TRAIN_DEV = 12
VAL_DEV = 4
HOPS = 3
TRAIN = 768
VAL = 256
LAYERS = 8
N_BLK = 64


def block_scale(own_key, dims, pieces, low, top_value):
    def one(position, shards_of):
        steps = jax.random.uniform(jax.random.fold_in(jax.random.fold_in(own_key, 6), position), (shards_of,), jnp.float32, low / len(pieces), top_value / len(pieces))
        return jnp.repeat(jnp.exp(steps), dims[position] // shards_of).reshape((-1,) + (1,) * (len(dims) - position - 1))

    factor_of = one(*pieces[0])
    for cut in pieces[1:]:
        factor_of = factor_of * one(*cut)
    return factor_of


def centred(rng, extent, deviation, limit, split=(), kind=jnp.bfloat16):
    level = block_scale(rng, extent, split, -0.22, 0.18) if split else 1.0
    values = jax.random.normal(rng, extent, jnp.float32) * deviation * level
    return jnp.minimum(jnp.maximum(values, -limit), limit).astype(kind)


def setup_inputs(seed: int = 0) -> dict:
    seeds = jax.random.split(jax.random.key(seed), 3)
    return {
        "train_factors": centred(seeds[0], (TRAIN, LAYERS, 2, TOK, R), 0.05, 0.29882812, ((0, 64), (1, 8))),
        "val_factors": centred(seeds[1], (VAL, LAYERS, 2, TOK, R), 0.05, 0.29882812, ((0, 64), (1, 8))),
    }


def pair_scores(train, val):
    train_f = train.astype(jnp.float32)
    val_f = val.astype(jnp.float32)
    act_gram = jnp.einsum('iltr,jlsr->ijlts', train_f[:, :, 0], val_f[:, :, 0])
    grad_gram = jnp.einsum('iltr,jlsr->ijlts', train_f[:, :, 1], val_f[:, :, 1])
    return jnp.sum(act_gram * grad_gram, axis=(2, 3, 4))


def reference(train_factors, val_factors):
    train_blocks = train_factors.reshape((N_BLK, TRAIN_DEV) + train_factors.shape[1:])
    val_blocks = val_factors.reshape((N_BLK, VAL_DEV) + val_factors.shape[1:])

    def one_block(index):
        train = lax.dynamic_index_in_dim(train_blocks, index, 0, keepdims=False)
        rows = []
        for hop in range(HOPS):
            source = ((index - hop) % N_BLK).astype(jnp.int32)
            val = lax.dynamic_index_in_dim(val_blocks, source, 0, keepdims=False)
            rows.append(pair_scores(train, val))
        return jnp.stack(rows, axis=1)

    result = lax.map(one_block, jnp.arange(N_BLK, dtype=jnp.int32))
    return result.reshape((N_BLK * TRAIN_DEV, HOPS, VAL_DEV))
```

```python
import jax
import jax.numpy as jnp
from jax import lax
from jax.experimental import pallas as pl
from jax.experimental.pallas import tpu as pltpu
from jax.sharding import PartitionSpec as P

MESH = pl.DeviceIdType.MESH
TRAIN_DEV = 12
VAL_DEV = 4
HOPS = 3
TOK = 64
R = 1024
LAYERS = 8
RING = 16
STEPS = 8
COLUMNS = 16
N_BLK = 64
OWN, SIBLING, FIRST = 0, 1, 2
ARRIVED = FIRST + STEPS - 1


def chip(column, z, core):
    column, z = lax.rem(column + COLUMNS, COLUMNS), lax.rem(z + RING, RING)
    return (column * 2 + z // LAYERS) * 2 + core, lax.rem(z, LAYERS)


def kernel(train, val, out, tokens, held, total, parts, load_sem, send_sem, recv_sem, sib_send, sib_recv, sum_send, sum_recv):
    blk, layer = lax.axis_index("blk"), lax.axis_index("layer")
    core, column = lax.rem(blk, 2), blk // 4
    z = lax.rem(blk // 2, 2) * LAYERS + layer
    target = (
        chip(column + (z == RING - 1).astype(jnp.int32), z + 1, core),
        chip(column + (z == LAYERS).astype(jnp.int32), z - 1, core),
    )
    source = (
        chip(column - (z == 0).astype(jnp.int32), z - 1, core),
        chip(column - (z == LAYERS - 1).astype(jnp.int32), z + 1, core),
    )
    sibling = (blk + 1 - 2 * core, layer)

    barrier = pltpu.get_barrier_semaphore()
    for device in (*source, sibling):
        pl.semaphore_signal(barrier, inc=1, device_id=device, device_id_type=MESH)
    pl.semaphore_wait(barrier, 3)

    def ring(step, d, p, g):
        rows = pl.ds(d * TOK, TOK)
        if isinstance(step, int) and step == 0:
            src = val.at[2 * d + p, g]
        else:
            src = held.at[FIRST + step - 1, p, g, rows]
        return pltpu.make_async_remote_copy(
            src,
            held.at[FIRST + step, p, g, rows],
            send_sem.at[step, d, p, g],
            recv_sem.at[step, d, p, g],
            device_id=target[d],
            device_id_type=MESH,
        )

    chunks = [(p, g) for p in range(2) for g in range(2)]
    for p, g in chunks:
        for d in range(2):
            ring(0, d, p, g).start()

    own = [
        pltpu.make_async_copy(
            val.at[2 * d + p, g], held.at[OWN, p, g, pl.ds(d * TOK, TOK)], load_sem.at[2 + d, p, g]
        )
        for p, g in chunks
        for d in range(2)
    ]
    for copy in own:
        copy.start()
    factors = [
        pltpu.make_async_copy(train.at[:, g], tokens.at[g], load_sem.at[0, 0, g]) for g in range(2)
    ]
    for copy in factors:
        copy.start()

    def to_sibling(slot, p, g):
        return pltpu.make_async_remote_copy(
            held.at[slot, p, g],
            held.at[SIBLING, p, g],
            sib_send.at[p, g],
            sib_recv.at[p, g],
            device_id=sibling,
            device_id_type=MESH,
        )

    total[...] = jnp.zeros_like(total)

    def gram(slot, p, g):
        return lax.dot_general(
            tokens[g].reshape(TRAIN_DEV * TOK, R),
            held[slot, p, g],
            (((1,), (1,)), ((), ())),
            preferred_element_type=jnp.float32,
        )

    def add_scores(slot, p, hop):
        product = gram(slot, p, 0) * gram(slot, p, 1)
        sums = jnp.sum(product.reshape(TRAIN_DEV, TOK, 2 * TOK), axis=1)
        lane = lax.broadcasted_iota(jnp.int32, sums.shape, 1)
        first = jnp.sum(jnp.where(lane < TOK, sums, 0.0), axis=1, keepdims=True)
        second = jnp.sum(jnp.where(lane < TOK, 0.0, sums), axis=1, keepdims=True)
        at = hop * VAL_DEV + p
        scores = jnp.where(lane == at, first, jnp.where(lane == at + 2, second, 0.0))
        total[pl.ds(0, TRAIN_DEV)] += scores

    for copy in own + factors:
        copy.wait()

    @pl.when(core == 0)
    def _():
        for p, g in chunks:
            to_sibling(OWN, p, g).start()

    def step_body(step, carry):
        for p, g in chunks:
            for d in range(2):
                ring(step - 1, d, p, g).wait_recv()
                ring(step, d, p, g).start()

        @pl.when(step >= 3)
        def _():
            for p, g in chunks:
                for d in range(2):
                    ring(step - 2, d, p, g).wait_send()

        @pl.when((core == 1) & (step == 3))
        def _():
            for p, g in chunks:
                to_sibling(OWN, p, g).wait_recv()

        @pl.when((step <= 2) | ((core == 1) & (step <= 4)))
        def _():
            turn = step - 1
            add_scores(turn // 2, lax.rem(turn, 2), turn // 2)

        return carry

    lax.fori_loop(1, STEPS, step_body, 0)

    for p in range(2):
        for g in range(2):
            for d in range(2):
                ring(STEPS - 1, d, p, g).wait_recv()

            @pl.when(core == 1)
            def _():
                to_sibling(ARRIVED, p, g).start()

        add_scores(ARRIVED, p, 2)

        @pl.when(core == 0)
        def _():
            for g in range(2):
                to_sibling(ARRIVED, p, g).wait_recv()
            add_scores(SIBLING, p, 1)

    parts[layer] = total[...]

    def share(peer):
        return pltpu.make_async_remote_copy(
            total,
            parts.at[layer],
            sum_send.at[peer],
            sum_recv.at[layer],
            device_id=(blk, peer),
            device_id_type=MESH,
        )

    def shared_by(peer):
        return pltpu.make_async_remote_copy(
            total,
            parts.at[peer],
            sum_send.at[peer],
            sum_recv.at[peer],
            device_id=(blk, peer),
            device_id_type=MESH,
        )

    for peer in range(LAYERS):

        @pl.when(peer != layer)
        def _():
            share(peer).start()

    for step in (0, STEPS - 2, STEPS - 1):
        for p, g in chunks:
            for d in range(2):
                ring(step, d, p, g).wait_send()
    for p, g in chunks:
        to_sibling(OWN, p, g).wait_send()

    for peer in range(LAYERS):

        @pl.when(peer != layer)
        def _():
            shared_by(peer).wait_recv()
            share(peer).wait_send()

    out[...] = jnp.sum(parts[...], axis=0)


def local(train_factors, val_factors):
    train = train_factors.reshape(TRAIN_DEV, 2, TOK, R)
    val = val_factors.reshape(VAL_DEV, 2, TOK, R)
    summed = pl.pallas_call(
        kernel,
        out_shape=jax.ShapeDtypeStruct((16, 128), jnp.float32),
        in_specs=[pl.BlockSpec(memory_space=pl.ANY)] * 2,
        out_specs=pl.BlockSpec(memory_space=pltpu.VMEM),
        scratch_shapes=[
            pltpu.VMEM((2, TRAIN_DEV, TOK, R), jnp.bfloat16),
            pltpu.VMEM((FIRST + STEPS, 2, 2, 2 * TOK, R), jnp.bfloat16),
            pltpu.VMEM((16, 128), jnp.float32),
            pltpu.VMEM((LAYERS, 16, 128), jnp.float32),
            pltpu.SemaphoreType.DMA((4, 2, 2)),
            pltpu.SemaphoreType.DMA((STEPS, 2, 2, 2)),
            pltpu.SemaphoreType.DMA((STEPS, 2, 2, 2)),
            pltpu.SemaphoreType.DMA((2, 2)),
            pltpu.SemaphoreType.DMA((2, 2)),
            pltpu.SemaphoreType.DMA((LAYERS,)),
            pltpu.SemaphoreType.DMA((LAYERS,)),
        ],
        compiler_params=pltpu.CompilerParams(
            collective_id=0, has_side_effects=True, vmem_limit_bytes=60 * 2**20
        ),
        name="score_ring",
    )(train, val)
    return summed[:TRAIN_DEV, : HOPS * VAL_DEV].reshape(TRAIN_DEV, HOPS, VAL_DEV)


def solution(mesh):
    return jax.shard_map(
        local,
        mesh=mesh,
        in_specs=(P("blk", "layer", None, None, None), P("blk", "layer", None, None, None)),
        out_specs=P("blk", None, None),
        check_vma=False,
    )
```

```python
import jax
import jax.numpy as jnp
from jax import lax
from jax.experimental import pallas as pl
from jax.experimental.pallas import tpu as pltpu
from jax.sharding import PartitionSpec as P

MESH = pl.DeviceIdType.MESH
TRAIN_DEV = 12
VAL_DEV = 4
HOPS = 3
TOK = 64
R = 1024
LAYERS = 8
RING = 16
STEPS = 8
COLUMNS = 16
SUMS = 16
OWN, SIBLING, FIRST = 0, 1, 2
ARRIVED = FIRST + STEPS - 1
UP, DOWN = 0, 1
CHUNKS = [(p, g) for p in range(2) for g in range(2)]
TURNED = [(1, 1)]


def chip(column, z, core):
    column, z = lax.rem(column + COLUMNS, COLUMNS), lax.rem(z + RING, RING)
    return (column * 2 + z // LAYERS) * 2 + core, lax.rem(z, LAYERS)


def kernel(
    train, val, out, tokens, held, turned, act_gram, total, parts,
    load_sem, send_sem, recv_sem, turned_send, turned_recv, sib_send, sib_recv, sum_send, sum_recv,
):
    blk, layer = lax.axis_index("blk"), lax.axis_index("layer")
    core, column = lax.rem(blk, 2), blk // 4
    z = lax.rem(blk // 2, 2) * LAYERS + layer
    sibling = (blk + 1 - 2 * core, layer)

    def target(step, d):
        if d == UP:
            crosses = ((z == 0) & (step >= 1)) | ((z == 9) & (step == 1))
            return chip(column + crosses.astype(jnp.int32), z + 1, core)
        crosses = ((z == 7) & (step >= 1)) | ((z == 14) & (step == 1))
        return chip(column + crosses.astype(jnp.int32), z - 1, core)

    barrier = pltpu.get_barrier_semaphore()

    def greet(device):
        pl.semaphore_signal(barrier, inc=1, device_id=device, device_id_type=MESH)

    greet(chip(column, z + 1, core))
    greet(chip(column, z - 1, core))
    greet(sibling)

    @pl.when((z == 1) | (z == 10))
    def _():
        greet(chip(column - 1, z - 1, core))

    @pl.when((z == 6) | (z == 13))
    def _():
        greet(chip(column - 1, z + 1, core))

    more = (z == 0) | (z == 9) | (z == 7) | (z == 14)
    pl.semaphore_wait(barrier, 3 + more.astype(jnp.int32))

    def ring(step, d, p, g):
        rows = pl.ds(d * TOK, TOK)
        if isinstance(step, int) and step == 0:
            src = val.at[2 * d + p, g]
        else:
            src = held.at[FIRST + step - 1, p, g, rows]
        return pltpu.make_async_remote_copy(
            src,
            held.at[FIRST + step, p, g, rows],
            send_sem.at[step, d, p, g],
            recv_sem.at[step, d, p, g],
            device_id=target(step, d),
            device_id_type=MESH,
        )

    def turn(which, step):
        p, g = TURNED[which]
        first = isinstance(step, int) and step == 0
        last = isinstance(step, int) and step == STEPS - 1
        return pltpu.make_async_remote_copy(
            val.at[2 + p, g] if first else turned.at[which],
            held.at[ARRIVED, p, g, pl.ds(TOK, TOK)] if last else turned.at[which],
            turned_send.at[which],
            turned_recv.at[which],
            device_id=target(step, UP),
            device_id_type=MESH,
        )

    def goes_down(step, p, g, use):
        if (p, g) in TURNED:
            pl.when(z + step != LAYERS)(use)
        else:
            use()

    def begin():
        for p, g in CHUNKS:
            ring(0, UP, p, g).start()
            goes_down(0, p, g, lambda: ring(0, DOWN, p, g).start())
        for which in range(len(TURNED)):
            pl.when(z == LAYERS)(lambda: turn(which, 0).start())

    @pl.when(core == 1)
    def _():
        begin()

    own = [
        pltpu.make_async_copy(
            val.at[2 * d + p, g], held.at[OWN, p, g, pl.ds(d * TOK, TOK)], load_sem.at[2 + d, p, g]
        )
        for p, g in CHUNKS
        for d in range(2)
    ]
    for copy in own:
        copy.start()
    @pl.when(core == 0)
    def _():
        for copy in own:
            copy.wait()
        begin()

    factors = [
        pltpu.make_async_copy(train.at[:, g], tokens.at[g], load_sem.at[0, 0, g]) for g in range(2)
    ]
    for copy in factors:
        copy.start()

    def to_sibling(slot, p, g):
        return pltpu.make_async_remote_copy(
            held.at[slot, p, g],
            held.at[SIBLING, p, g],
            sib_send.at[p, g],
            sib_recv.at[p, g],
            device_id=sibling,
            device_id_type=MESH,
        )

    total[...] = jnp.zeros_like(total)

    def gram(g, left, right):
        return lax.dot_general(
            tokens[g].reshape(TRAIN_DEV * TOK, R),
            jnp.concatenate([left[...], right[...]], axis=0),
            (((1,), (1,)), ((), ())),
            preferred_element_type=jnp.float32,
        )

    def put_scores(act, grad, rows):
        sums = jnp.sum((act * grad).reshape(TRAIN_DEV, TOK, 4 * TOK), axis=1)
        sums = jnp.concatenate([sums, jnp.zeros((SUMS - TRAIN_DEV, 4 * TOK), jnp.float32)], axis=0)
        sums = jnp.sum(sums.T.reshape(4, TOK, SUMS), axis=1)
        for i, row in enumerate(rows):
            total[row : row + 1, pl.ds(0, SUMS)] = sums[i : i + 1]

    @pl.when(core == 1)
    def _():
        for copy in own:
            copy.wait()

    for copy in factors:
        copy.wait()

    @pl.when(core == 0)
    def _():
        for p, g in CHUNKS:
            to_sibling(OWN, p, g).start()

    put_scores(*(gram(g, held.at[OWN, 0, g], held.at[OWN, 1, g]) for g in range(2)), (0, 2, 1, 3))

    def step_body(step, carry):
        for p, g in CHUNKS:
            ring(step - 1, UP, p, g).wait_recv()
            ring(step, UP, p, g).start()

            def pass_down():
                ring(step - 1, DOWN, p, g).wait_recv()
                ring(step, DOWN, p, g).start()

            goes_down(step, p, g, pass_down)

        for which in range(len(TURNED)):

            @pl.when(z == LAYERS + step)
            def _():
                turn(which, 0).wait_recv()

                @pl.when(step < STEPS - 1)
                def _():
                    turn(which, step).start()

                @pl.when(step == STEPS - 1)
                def _():
                    turn(which, STEPS - 1).start()

        @pl.when(step >= 3)
        def _():
            for p, g in CHUNKS:
                ring(step - 2, UP, p, g).wait_send()
                goes_down(step - 2, p, g, lambda: ring(step - 2, DOWN, p, g).wait_send())

        return carry

    lax.fori_loop(1, STEPS, step_body, 0)

    def arrive(p, g):
        ring(STEPS - 1, UP, p, g).wait_recv()
        goes_down(STEPS, p, g, lambda: ring(STEPS - 1, DOWN, p, g).wait_recv())
        if (p, g) in TURNED:
            pl.when(z == 0)(lambda: turn(TURNED.index((p, g)), STEPS - 1).wait_recv())

    for p in range(2):
        for g in range(2):

            @pl.when(core == 1)
            def _():
                arrive(p, g)
                to_sibling(ARRIVED, p, g).start()
                to_sibling(OWN, p, g).wait_recv()

            @pl.when(core == 0)
            def _():
                to_sibling(ARRIVED, p, g).wait_recv()
                arrive(p, g)

            left, right = held.at[SIBLING, p, g], held.at[ARRIVED, p, g]
            if g == 0:
                act_gram[...] = gram(g, left, right)
            else:
                one, two = VAL_DEV + p, 2 * VAL_DEV + p
                put_scores(act_gram[...], gram(g, left, right), (one, one + 2, two, two + 2))

    parts[layer] = total[...]

    def share(peer, sender):
        return pltpu.make_async_remote_copy(
            total,
            parts.at[sender],
            sum_send.at[peer],
            sum_recv.at[sender],
            device_id=(blk, peer),
            device_id_type=MESH,
        )

    for peer in range(LAYERS):

        @pl.when(peer != layer)
        def _():
            share(peer, layer).start()

    for step in (0, STEPS - 2, STEPS - 1):
        for p, g in CHUNKS:
            ring(step, UP, p, g).wait_send()
            goes_down(step, p, g, lambda: ring(step, DOWN, p, g).wait_send())
    for p, g in CHUNKS:
        to_sibling(OWN, p, g).wait_send()
    for which in range(len(TURNED)):
        pl.when(z >= LAYERS)(lambda: turn(which, 0).wait_send())

    for peer in range(LAYERS):

        @pl.when(peer != layer)
        def _():
            share(peer, peer).wait_recv()
            share(peer, layer).wait_send()

    out[...] = jnp.sum(parts[...], axis=0)


def local(train_factors, val_factors):
    train = train_factors.reshape(TRAIN_DEV, 2, TOK, R)
    val = val_factors.reshape(VAL_DEV, 2, TOK, R)
    summed = pl.pallas_call(
        kernel,
        out_shape=jax.ShapeDtypeStruct((SUMS, 128), jnp.float32),
        in_specs=[pl.BlockSpec(memory_space=pl.ANY)] * 2,
        out_specs=pl.BlockSpec(memory_space=pltpu.VMEM),
        scratch_shapes=[
            pltpu.VMEM((2, TRAIN_DEV, TOK, R), jnp.bfloat16),
            pltpu.VMEM((FIRST + STEPS, 2, 2, 2 * TOK, R), jnp.bfloat16),
            pltpu.VMEM((max(len(TURNED), 1), TOK, R), jnp.bfloat16),
            pltpu.VMEM((TRAIN_DEV * TOK, 4 * TOK), jnp.float32),
            pltpu.VMEM((SUMS, 128), jnp.float32),
            pltpu.VMEM((LAYERS, SUMS, 128), jnp.float32),
            pltpu.SemaphoreType.DMA((4, 2, 2)),
            pltpu.SemaphoreType.DMA((STEPS, 2, 2, 2)),
            pltpu.SemaphoreType.DMA((STEPS, 2, 2, 2)),
            pltpu.SemaphoreType.DMA((max(len(TURNED), 1),)),
            pltpu.SemaphoreType.DMA((max(len(TURNED), 1),)),
            pltpu.SemaphoreType.DMA((2, 2)),
            pltpu.SemaphoreType.DMA((2, 2)),
            pltpu.SemaphoreType.DMA((LAYERS,)),
            pltpu.SemaphoreType.DMA((LAYERS,)),
        ],
        compiler_params=pltpu.CompilerParams(
            collective_id=0, has_side_effects=True, vmem_limit_bytes=60 * 2**20
        ),
        name="score_ring",
    )(train, val)
    scores = summed[: HOPS * VAL_DEV, :TRAIN_DEV]
    return scores.reshape(HOPS, VAL_DEV, TRAIN_DEV).transpose(2, 0, 1)


def solution(mesh):
    return jax.shard_map(
        local,
        mesh=mesh,
        in_specs=(P("blk", "layer", None, None, None), P("blk", "layer", None, None, None)),
        out_specs=P("blk", None, None),
        check_vma=False,
    )
```

```python
import jax
import jax.numpy as jnp
from jax import lax
from jax.experimental import pallas as pl
from jax.experimental.pallas import tpu as pltpu
from jax.sharding import PartitionSpec as P

MESH = pl.DeviceIdType.MESH
TRAIN_DEV = 12
VAL_DEV = 4
HOPS = 3
TOK = 64
R = 1024
LAYERS = 8
RING = 16
LAST = 7
COLUMNS = 16
SUMS = 16
UP, DOWN = 0, 1
OWN, OTHER = 0, 1
CHUNKS = [(p, g) for p in range(2) for g in range(2)]
TURNED = {UP: [(1, 0), (1, 1)], DOWN: [(1, 1)]}
TURN_AT = {UP: LAYERS, DOWN: RING - 1}
TURNS = max(len(TURNED[UP]), len(TURNED[DOWN]), 1)
HEAD = 2
ORDER = {UP: [(OWN, 0, 0), (OWN, 0, 1), (OTHER, 0, 0), (OTHER, 0, 1), (OTHER, 1, 0), (OTHER, 1, 1), (OWN, 1, 0), (OWN, 1, 1)], DOWN: [(OWN, 0, 0), (OWN, 0, 1), (OTHER, 0, 0), (OTHER, 0, 1), (OWN, 1, 0), (OWN, 1, 1), (OTHER, 1, 0), (OTHER, 1, 1)]}


def chip(column, z, core):
    column, z = lax.rem(column + COLUMNS, COLUMNS), lax.rem(z + RING, RING)
    return (column * 2 + z // LAYERS) * 2 + core, lax.rem(z, LAYERS)


def quarter(i):
    return pl.ds(i * TOK, TOK)


def kernel(
    train, val, out, tokens, own, held, last, turned, act_gram, total, parts, load_sem, stage_send, stage_recv, give_send,
    give_recv, send_sem, recv_sem, cross_recv, turned_send, turned_recv, pass_send, pass_recv, sum_send, sum_recv,
):
    blk, layer = lax.axis_index("blk"), lax.axis_index("layer")
    core, column = lax.rem(blk, 2), blk // 4
    z = lax.rem(blk // 2, 2) * LAYERS + layer
    sibling = (blk + 1 - 2 * core, layer)

    def remote(src, dst, sent, received, device):
        return pltpu.make_async_remote_copy(src, dst, sent, received, device_id=device, device_id_type=MESH)

    def target(step, d, on_core):
        if d == UP:
            crosses = ((z == 0) & (step >= 1)) | ((z == 9) & (step == 1))
            return chip(column + crosses.astype(jnp.int32), z + 1, on_core)
        crosses = ((z == 7) & (step >= 1)) | ((z == 14) & (step == 1))
        return chip(column + crosses.astype(jnp.int32), z - 1, on_core)

    barrier = pltpu.get_barrier_semaphore()

    def greet(device):
        pl.semaphore_signal(barrier, inc=1, device_id=device, device_id_type=MESH)

    @pl.when(core == 0)
    def _():
        greet(chip(column, z - 1, 0))
        greet(chip(column, z + 1, 1))

        @pl.when((z == 1) | (z == 10))
        def _():
            greet(chip(column - 1, z - 1, 0))

        @pl.when(z == 6)
        def _():
            greet(chip(column - 1, z + 1, 1))

    @pl.when(core == 1)
    def _():
        greet(chip(column, z + 1, 1))

        @pl.when((z == 6) | (z == 13))
        def _():
            greet(chip(column - 1, z + 1, 1))

    greet(sibling)
    more_up = (core == 0) & ((z == 0) | (z == 9))
    more_down = (core == 1) & ((z == 7) | (z == 14))
    last_down = (core == 1) & (z == 7)
    pl.semaphore_wait(
        barrier,
        2 + core + more_up.astype(jnp.int32) + more_down.astype(jnp.int32) + last_down.astype(jnp.int32),
    )

    def ring(step, d, which, p, g):
        first = isinstance(step, int) and step == 0
        src = val.at[2 * d + p, g] if first and which == OWN else held.at[step, which, p, g]
        on_core, received = d, recv_sem.at[step, which, p, g]
        if isinstance(step, int) and step == LAST:
            dst = last.at[p, g, quarter((2 if which == d else 0) + d)]
            if d == DOWN and which == OTHER:
                on_core, received = 0, cross_recv.at[p, g]
        else:
            dst = held.at[step + 1, which, p, g]
        return remote(src, dst, send_sem.at[step, which, p, g], received, target(step, d, on_core))

    def starts_at(step, d):
        return lax.rem(z - step + RING, RING) if d == UP else lax.rem(z + step, RING)

    def unless_turned(step, d, which, p, g, use):
        other_way = 1 - d
        if which == d and (p, g) in TURNED[other_way]:
            pl.when(starts_at(step, d) != TURN_AT[other_way])(use)
        else:
            use()

    def turn(i, step, d):
        p, g = TURNED[d][i]
        first = isinstance(step, int) and step == 0
        ends = isinstance(step, int) and step == LAST
        here = last.at[p, g, quarter(3 if d == UP else 2)]
        if first:
            src = val.at[2 + p, g] if d == UP else here
        else:
            src = turned.at[i]
        return remote(
            src, here if ends else turned.at[i], turned_send.at[i], turned_recv.at[i], target(step, d, 0 if ends else d)
        )

    def stage(p, g):
        half = 2 * (1 - core) + p
        return remote(val.at[half, g], held.at[0, OTHER, p, g], stage_send.at[p, g], stage_recv.at[p, g], sibling)

    def give(p, g, d):
        return remote(
            val.at[2 * d + p, g], last.at[p, g, quarter(2 + d)], give_send.at[p, g, d], give_recv.at[p, g, d], sibling
        )

    def hand_over(d, p, g):
        here = last.at[p, g, quarter(d)]
        return remote(here, here, pass_send.at[p, g], pass_recv.at[p, g], sibling)

    for d in range(2):

        @pl.when(core == d)
        def _():
            for which, p, g in ORDER[d][:HEAD]:
                unless_turned(0, d, which, p, g, lambda: ring(0, d, which, p, g).start())

    for p, g in CHUNKS:
        stage(p, g).start()
    loads = [pltpu.make_async_copy(val.at[:, g], own.at[g], load_sem.at[0, g]) for g in range(2)]
    loads += [pltpu.make_async_copy(train.at[:, g], tokens.at[g], load_sem.at[1, g]) for g in range(2)]
    for copy in loads:
        copy.start()

    for d in range(2):

        @pl.when(core == d)
        def _():
            for which, p, g in ORDER[d][HEAD:]:
                if which == OTHER:
                    stage(p, g).wait_recv()
                unless_turned(0, d, which, p, g, lambda: ring(0, d, which, p, g).start())
            if d == UP:
                for i in range(len(TURNED[UP])):
                    pl.when(z == TURN_AT[UP])(lambda: turn(i, 0, UP).start())
                for half in range(2):
                    for p, g in CHUNKS:
                        give(p, g, half).start()
            else:
                for p, g in CHUNKS:
                    give(p, g, 0).wait_recv()
                for i in range(len(TURNED[DOWN])):
                    pl.when(z == TURN_AT[DOWN])(lambda: turn(i, 0, DOWN).start())

    total[...] = jnp.zeros_like(total)

    def gram(g, rows):
        return lax.dot_general(
            tokens[g].reshape(TRAIN_DEV * TOK, R),
            rows,
            (((1,), (1,)), ((), ())),
            preferred_element_type=jnp.float32,
        )

    def put_scores(act, grad, rows):
        sums = jnp.sum((act * grad).reshape(TRAIN_DEV, TOK, 4 * TOK), axis=1)
        sums = jnp.concatenate([sums, jnp.zeros((SUMS - TRAIN_DEV, 4 * TOK), jnp.float32)], axis=0)
        sums = jnp.sum(sums.T.reshape(4, TOK, SUMS), axis=1)
        for i, row in enumerate(rows):
            total[pl.ds(row, 1), pl.ds(0, SUMS)] = sums[i : i + 1]

    for copy in loads:
        copy.wait()
    put_scores(*(gram(g, own[g].reshape(4 * TOK, R)) for g in range(2)), range(VAL_DEV))

    for d in range(2):

        @pl.when(core == d)
        def _():
            def step_body(step, carry):
                for which, p, g in ORDER[d]:

                    def send_on():
                        ring(step - 1, d, which, p, g).wait_recv()
                        ring(step, d, which, p, g).start()

                    unless_turned(step, d, which, p, g, send_on)
                for i in range(len(TURNED[d])):

                    @pl.when((starts_at(step, d) == TURN_AT[d]) & (z >= LAYERS))
                    def _():
                        turn(i, step, d).wait_recv()
                        turn(i, step, d).start()

                @pl.when(step >= 3)
                def _():
                    for which, p, g in ORDER[d]:
                        unless_turned(step - 2, d, which, p, g, lambda: ring(step - 2, d, which, p, g).wait_send())

                return carry

            lax.fori_loop(1, LAST, step_body, 0)
            for which, p, g in ORDER[d]:

                def send_on():
                    ring(LAST - 1, d, which, p, g).wait_recv()
                    ring(LAST, d, which, p, g).start()

                unless_turned(LAST, d, which, p, g, send_on)
            for i in range(len(TURNED[d])):

                @pl.when(z == (TURN_AT[d] + (LAST if d == UP else -LAST)))
                def _():
                    turn(i, 1, d).wait_recv()
                    turn(i, LAST, d).start()

    for p in range(2):

        @pl.when(core == 0)
        def _():
            for g in range(2):
                ring(LAST, UP, OTHER, p, g).wait_recv()
                hand_over(UP, p, g).start()

        @pl.when(core == 1)
        def _():
            for g in range(2):
                ring(LAST, DOWN, OWN, p, g).wait_recv()
                hand_over(DOWN, p, g).start()

        for g in range(2):

            @pl.when(core == 0)
            def _():
                hand_over(DOWN, p, g).wait_recv()
                for way in (DOWN, UP):
                    which = OTHER if way == DOWN else OWN
                    other_way = 1 - way
                    if (p, g) in TURNED[other_way]:
                        ends = 0 if other_way == UP else LAYERS - 1
                        i = TURNED[other_way].index((p, g))
                        pl.when(z == ends)(lambda: turn(i, LAST, other_way).wait_recv())
                        pl.when(z != ends)(lambda: ring(LAST, way, which, p, g).wait_recv())
                    else:
                        ring(LAST, way, which, p, g).wait_recv()

            @pl.when(core == 1)
            def _():
                hand_over(UP, p, g).wait_recv()
                give(p, g, 1).wait_recv()

            if g == 0:
                act_gram[...] = gram(g, last[p, g])
            else:
                one, two = (1 + core) * VAL_DEV + p, (2 - core) * VAL_DEV + p
                put_scores(act_gram[...], gram(g, last[p, g]), (one, one + 2, two, two + 2))

    parts[layer] = total[...]

    def share(peer, sender):
        return remote(total, parts.at[sender], sum_send.at[peer], sum_recv.at[sender], (blk, peer))

    for peer in range(LAYERS):

        @pl.when(peer != layer)
        def _():
            share(peer, layer).start()

    for d in range(2):

        @pl.when(core == d)
        def _():
            for step in (0, LAST - 2, LAST - 1, LAST):
                for which, p, g in ORDER[d]:
                    unless_turned(step, d, which, p, g, lambda: ring(step, d, which, p, g).wait_send())
            for p, g in CHUNKS:
                hand_over(d, p, g).wait_send()
            if d == UP:
                for p, g in CHUNKS:
                    for half in range(2):
                        give(p, g, half).wait_send()
            for i in range(len(TURNED[d])):
                pl.when(z >= LAYERS)(lambda: turn(i, 0, d).wait_send())

    for p, g in CHUNKS:
        stage(p, g).wait_send()

    for peer in range(LAYERS):

        @pl.when(peer != layer)
        def _():
            share(peer, peer).wait_recv()
            share(peer, layer).wait_send()

    out[...] = jnp.sum(parts[...], axis=0)


def local(train_factors, val_factors):
    train = train_factors.reshape(TRAIN_DEV, 2, TOK, R)
    val = val_factors.reshape(VAL_DEV, 2, TOK, R)
    dma = pltpu.SemaphoreType.DMA
    summed = pl.pallas_call(
        kernel,
        out_shape=jax.ShapeDtypeStruct((SUMS, 128), jnp.float32),
        in_specs=[pl.BlockSpec(memory_space=pl.ANY)] * 2,
        out_specs=pl.BlockSpec(memory_space=pltpu.VMEM),
        scratch_shapes=[
            pltpu.VMEM((2, TRAIN_DEV, TOK, R), jnp.bfloat16),
            pltpu.VMEM((2, VAL_DEV, TOK, R), jnp.bfloat16),
            pltpu.VMEM((LAST + 1, 2, 2, 2, TOK, R), jnp.bfloat16),
            pltpu.VMEM((2, 2, 4 * TOK, R), jnp.bfloat16),
            pltpu.VMEM((TURNS, TOK, R), jnp.bfloat16),
            pltpu.VMEM((TRAIN_DEV * TOK, 4 * TOK), jnp.float32),
            pltpu.VMEM((SUMS, 128), jnp.float32),
            pltpu.VMEM((LAYERS, SUMS, 128), jnp.float32),
            dma((2, 2)),
            dma((2, 2)),
            dma((2, 2)),
            dma((2, 2, 2)),
            dma((2, 2, 2)),
            dma((LAST + 1, 2, 2, 2)),
            dma((LAST + 1, 2, 2, 2)),
            dma((2, 2)),
            dma((TURNS,)),
            dma((TURNS,)),
            dma((2, 2)),
            dma((2, 2)),
            dma((LAYERS,)),
            dma((LAYERS,)),
        ],
        compiler_params=pltpu.CompilerParams(
            collective_id=0, has_side_effects=True, vmem_limit_bytes=60 * 2**20
        ),
        name="score_ring",
    )(train, val)
    scores = summed[: HOPS * VAL_DEV, :TRAIN_DEV]
    return scores.reshape(HOPS, VAL_DEV, TRAIN_DEV).transpose(2, 0, 1)


def solution(mesh):
    return jax.shard_map(
        local,
        mesh=mesh,
        in_specs=(P("blk", "layer", None, None, None), P("blk", "layer", None, None, None)),
        out_specs=P("blk", None, None),
        check_vma=False,
    )
```

```python
import jax
import jax.numpy as jnp
from jax import lax
from jax.experimental import pallas as pl
from jax.experimental.pallas import tpu as pltpu
from jax.sharding import PartitionSpec as P

MESH = pl.DeviceIdType.MESH
TRAIN_DEV = 12
VAL_DEV = 4
HOPS = 3
TOK = 64
R = 1024
LAYERS = 8
RING = 16
LAST = 7
COLUMNS = 16
SUMS = 16
UP, DOWN = 0, 1
OWN, OTHER = 0, 1
CHUNKS = [(p, g) for p in range(2) for g in range(2)]
TURNED = {UP: [(0, 1), (1, 0), (1, 1)], DOWN: [(1, 0), (1, 1)]}
TURN_AT = {UP: LAYERS, DOWN: RING - 1}
TURNS = max(len(TURNED[UP]), len(TURNED[DOWN]), 1)
HEAD = 1
ORDER = {UP: [(OWN, 0), (OTHER, 0), (OTHER, 1), (OWN, 1)], DOWN: [(OWN, 0), (OTHER, 0), (OWN, 1), (OTHER, 1)]}
BOTH = pl.ds(0, 2)


def chip(column, z, core):
    column, z = lax.rem(column + COLUMNS, COLUMNS), lax.rem(z + RING, RING)
    return (column * 2 + z // LAYERS) * 2 + core, lax.rem(z, LAYERS)


def quarter(i):
    return pl.ds(i * TOK, TOK)


def kernel(
    train, val, out, tokens, own, held, last, turned, act_gram, total, parts, load_sem, stage_send, stage_recv, give_send,
    give_recv, send_sem, recv_sem, cross_recv, turned_send, turned_recv, pass_send, pass_recv, sum_send, sum_recv,
):
    blk, layer = lax.axis_index("blk"), lax.axis_index("layer")
    core, column = lax.rem(blk, 2), blk // 4
    z = lax.rem(blk // 2, 2) * LAYERS + layer
    sibling = (blk + 1 - 2 * core, layer)

    def remote(src, dst, sent, received, device):
        return pltpu.make_async_remote_copy(src, dst, sent, received, device_id=device, device_id_type=MESH)

    def target(step, d, on_core):
        if d == UP:
            crosses = ((z == 0) & (step >= 1)) | ((z == 9) & (step == 1))
            return chip(column + crosses.astype(jnp.int32), z + 1, on_core)
        crosses = ((z == 7) & (step >= 1)) | ((z == 14) & (step == 1))
        return chip(column + crosses.astype(jnp.int32), z - 1, on_core)

    barrier = pltpu.get_barrier_semaphore()

    def greet(device):
        pl.semaphore_signal(barrier, inc=1, device_id=device, device_id_type=MESH)

    @pl.when(core == 0)
    def _():
        greet(chip(column, z - 1, 0))
        greet(chip(column, z + 1, 1))

        @pl.when((z == 1) | (z == 10))
        def _():
            greet(chip(column - 1, z - 1, 0))

        @pl.when(z == 6)
        def _():
            greet(chip(column - 1, z + 1, 1))

    @pl.when(core == 1)
    def _():
        greet(chip(column, z + 1, 1))

        @pl.when((z == 6) | (z == 13))
        def _():
            greet(chip(column - 1, z + 1, 1))

    greet(sibling)
    more_up = (core == 0) & ((z == 0) | (z == 9))
    more_down = (core == 1) & ((z == 7) | (z == 14))
    last_down = (core == 1) & (z == 7)
    pl.semaphore_wait(
        barrier,
        2 + core + more_up.astype(jnp.int32) + more_down.astype(jnp.int32) + last_down.astype(jnp.int32),
    )

    def ring(step, d, which, p, g):
        first = isinstance(step, int) and step == 0
        src = val.at[2 * d + p, g] if first and which == OWN else held.at[step, which, p, g]
        sem = 1 if isinstance(g, int) else 0
        on_core, received = d, recv_sem.at[step, which, p, sem]
        if isinstance(step, int) and step == LAST:
            dst = last.at[p, g, quarter((2 if which == d else 0) + d)]
            received = recv_sem.at[step, which, p, g]
            sem = g
            if d == DOWN and which == OTHER:
                on_core, received = 0, cross_recv.at[p, g]
        else:
            dst = held.at[step + 1, which, p, g]
        return remote(src, dst, send_sem.at[step, which, p, sem], received, target(step, d, on_core))

    def starts_at(step, d):
        return lax.rem(z - step + RING, RING) if d == UP else lax.rem(z + step, RING)

    def goes(step, d, which, p, use):
        left = [g for g in range(2) if which != d or (p, g) not in TURNED[1 - d]]
        if len(left) == 2:
            use(BOTH)
        else:
            turns = starts_at(step, d) == TURN_AT[1 - d]
            pl.when(jnp.logical_not(turns))(lambda: use(BOTH))
            for g in left:
                pl.when(turns)(lambda: use(g))

    def ends(step, d, which, p, g, use):
        if which == d and (p, g) in TURNED[1 - d]:
            pl.when(starts_at(step, d) != TURN_AT[1 - d])(use)
        else:
            use()

    def turn(i, step, d):
        p, g = TURNED[d][i]
        first = isinstance(step, int) and step == 0
        final = isinstance(step, int) and step == LAST
        here = last.at[p, g, quarter(3 if d == UP else 2)]
        if first:
            src = val.at[2 + p, g] if d == UP else here
        else:
            src = turned.at[i]
        return remote(
            src, here if final else turned.at[i], turned_send.at[i], turned_recv.at[i], target(step, d, 0 if final else d)
        )

    def stage(p):
        half = 2 * (1 - core) + p
        return remote(val.at[half], held.at[0, OTHER, p], stage_send.at[p], stage_recv.at[p], sibling)

    def give(p, g, d):
        return remote(
            val.at[2 * d + p, g], last.at[p, g, quarter(2 + d)], give_send.at[p, g, d], give_recv.at[p, g, d], sibling
        )

    def hand_over(d, p, g):
        here = last.at[p, g, quarter(d)]
        return remote(here, here, pass_send.at[p, g], pass_recv.at[p, g], sibling)

    for d in range(2):

        @pl.when(core == d)
        def _():
            for which, p in ORDER[d][:HEAD]:
                goes(0, d, which, p, lambda g: ring(0, d, which, p, g).start())

    for p in range(2):
        stage(p).start()
    loads = [pltpu.make_async_copy(val.at[:, g], own.at[g], load_sem.at[0, g]) for g in range(2)]
    loads += [pltpu.make_async_copy(train.at[:, g], tokens.at[g], load_sem.at[1, g]) for g in range(2)]
    for copy in loads:
        copy.start()

    for d in range(2):

        @pl.when(core == d)
        def _():
            for which, p in ORDER[d][HEAD:]:
                if which == OTHER:
                    stage(p).wait_recv()
                goes(0, d, which, p, lambda g: ring(0, d, which, p, g).start())
            if d == UP:
                for i in range(len(TURNED[UP])):
                    pl.when(z == TURN_AT[UP])(lambda: turn(i, 0, UP).start())
                for half in range(2):
                    for p, g in CHUNKS:
                        give(p, g, half).start()
            else:
                for p, g in CHUNKS:
                    give(p, g, 0).wait_recv()
                for i in range(len(TURNED[DOWN])):
                    pl.when(z == TURN_AT[DOWN])(lambda: turn(i, 0, DOWN).start())

    total[...] = jnp.zeros_like(total)

    def gram(g, rows):
        return lax.dot_general(
            tokens[g].reshape(TRAIN_DEV * TOK, R),
            rows,
            (((1,), (1,)), ((), ())),
            preferred_element_type=jnp.float32,
        )

    def put_scores(act, grad, rows):
        sums = jnp.sum((act * grad).reshape(TRAIN_DEV, TOK, 4 * TOK), axis=1)
        sums = jnp.concatenate([sums, jnp.zeros((SUMS - TRAIN_DEV, 4 * TOK), jnp.float32)], axis=0)
        sums = jnp.sum(sums.T.reshape(4, TOK, SUMS), axis=1)
        for i, row in enumerate(rows):
            total[pl.ds(row, 1), pl.ds(0, SUMS)] = sums[i : i + 1]

    for copy in loads:
        copy.wait()
    put_scores(*(gram(g, own[g].reshape(4 * TOK, R)) for g in range(2)), range(VAL_DEV))

    for d in range(2):

        @pl.when(core == d)
        def _():
            def step_body(step, carry):
                for which, p in ORDER[d]:

                    def send_on(g):
                        ring(step - 1, d, which, p, g).wait_recv()
                        ring(step, d, which, p, g).start()

                    goes(step, d, which, p, send_on)
                for i in range(len(TURNED[d])):

                    @pl.when((starts_at(step, d) == TURN_AT[d]) & (z >= LAYERS))
                    def _():
                        turn(i, step, d).wait_recv()
                        turn(i, step, d).start()

                @pl.when(step >= 3)
                def _():
                    for which, p in ORDER[d]:
                        goes(step - 2, d, which, p, lambda g: ring(step - 2, d, which, p, g).wait_send())

                return carry

            lax.fori_loop(1, LAST, step_body, 0)
            for which, p in ORDER[d]:
                goes(LAST, d, which, p, lambda g: ring(LAST - 1, d, which, p, g).wait_recv())
                for g in range(2):
                    ends(LAST, d, which, p, g, lambda: ring(LAST, d, which, p, g).start())
            for i in range(len(TURNED[d])):

                @pl.when(z == (TURN_AT[d] + (LAST if d == UP else -LAST)))
                def _():
                    turn(i, 1, d).wait_recv()
                    turn(i, LAST, d).start()

    def pass_on(d, p):
        for g in range(2):
            ring(LAST, d, OTHER if d == UP else OWN, p, g).wait_recv()
            hand_over(d, p, g).start()

    for p in range(2):

        @pl.when((core == 0) & ((z != 0) if p else (z >= 0)))
        def _():
            pass_on(UP, p)

        if p == 0:
            @pl.when((core == 0) & (z == 0))
            def _():
                pass_on(UP, 1)

        @pl.when(core == 1)
        def _():
            pass_on(DOWN, p)

        for g in range(2):

            @pl.when(core == 0)
            def _():
                hand_over(DOWN, p, g).wait_recv()
                for way in (DOWN, UP):
                    which = OTHER if way == DOWN else OWN
                    other_way = 1 - way
                    if (p, g) in TURNED[other_way]:
                        ends = 0 if other_way == UP else LAYERS - 1
                        i = TURNED[other_way].index((p, g))
                        pl.when(z == ends)(lambda: turn(i, LAST, other_way).wait_recv())
                        pl.when(z != ends)(lambda: ring(LAST, way, which, p, g).wait_recv())
                    else:
                        ring(LAST, way, which, p, g).wait_recv()

            @pl.when(core == 1)
            def _():
                hand_over(UP, p, g).wait_recv()
                give(p, g, 1).wait_recv()

            if g == 0:
                act_gram[...] = gram(g, last[p, g])
            else:
                one, two = (1 + core) * VAL_DEV + p, (2 - core) * VAL_DEV + p
                put_scores(act_gram[...], gram(g, last[p, g]), (one, one + 2, two, two + 2))

    parts[layer] = total[...]

    def share(peer, sender):
        return remote(total, parts.at[sender], sum_send.at[peer], sum_recv.at[sender], (blk, peer))

    for peer in range(LAYERS):

        @pl.when(peer != layer)
        def _():
            share(peer, layer).start()

    for d in range(2):

        @pl.when(core == d)
        def _():
            for which, p in ORDER[d]:
                for step in (0, LAST - 2, LAST - 1):
                    goes(step, d, which, p, lambda g: ring(step, d, which, p, g).wait_send())
                for g in range(2):
                    ends(LAST, d, which, p, g, lambda: ring(LAST, d, which, p, g).wait_send())
            for p, g in CHUNKS:
                hand_over(d, p, g).wait_send()
            if d == UP:
                for p, g in CHUNKS:
                    for half in range(2):
                        give(p, g, half).wait_send()
            for i in range(len(TURNED[d])):
                pl.when(z >= LAYERS)(lambda: turn(i, 0, d).wait_send())

    for p in range(2):
        stage(p).wait_send()

    for peer in range(LAYERS):

        @pl.when(peer != layer)
        def _():
            share(peer, peer).wait_recv()
            share(peer, layer).wait_send()

    out[...] = jnp.sum(parts[...], axis=0)


def local(train_factors, val_factors):
    train = train_factors.reshape(TRAIN_DEV, 2, TOK, R)
    val = val_factors.reshape(VAL_DEV, 2, TOK, R)
    dma = pltpu.SemaphoreType.DMA
    summed = pl.pallas_call(
        kernel,
        out_shape=jax.ShapeDtypeStruct((SUMS, 128), jnp.float32),
        in_specs=[pl.BlockSpec(memory_space=pl.ANY)] * 2,
        out_specs=pl.BlockSpec(memory_space=pltpu.VMEM),
        scratch_shapes=[
            pltpu.VMEM((2, TRAIN_DEV, TOK, R), jnp.bfloat16),
            pltpu.VMEM((2, VAL_DEV, TOK, R), jnp.bfloat16),
            pltpu.VMEM((LAST + 1, 2, 2, 2, TOK, R), jnp.bfloat16),
            pltpu.VMEM((2, 2, 4 * TOK, R), jnp.bfloat16),
            pltpu.VMEM((TURNS, TOK, R), jnp.bfloat16),
            pltpu.VMEM((TRAIN_DEV * TOK, 4 * TOK), jnp.float32),
            pltpu.VMEM((SUMS, 128), jnp.float32),
            pltpu.VMEM((LAYERS, SUMS, 128), jnp.float32),
            dma((2, 2)),
            dma((2,)),
            dma((2,)),
            dma((2, 2, 2)),
            dma((2, 2, 2)),
            dma((LAST + 1, 2, 2, 2)),
            dma((LAST + 1, 2, 2, 2)),
            dma((2, 2)),
            dma((TURNS,)),
            dma((TURNS,)),
            dma((2, 2)),
            dma((2, 2)),
            dma((LAYERS,)),
            dma((LAYERS,)),
        ],
        compiler_params=pltpu.CompilerParams(
            collective_id=0, has_side_effects=True, vmem_limit_bytes=53 * 2**20
        ),
        name="score_ring",
    )(train, val)
    scores = summed[: HOPS * VAL_DEV, :TRAIN_DEV]
    return scores.reshape(HOPS, VAL_DEV, TRAIN_DEV).transpose(2, 0, 1)


def solution(mesh):
    return jax.shard_map(
        local,
        mesh=mesh,
        in_specs=(P("blk", "layer", None, None, None), P("blk", "layer", None, None, None)),
        out_specs=P("blk", None, None),
        check_vma=False,
    )
```

```python
import jax
import jax.numpy as jnp
from jax import lax
from jax.experimental import pallas as pl
from jax.experimental.pallas import tpu as pltpu
from jax.sharding import PartitionSpec as P

MESH = pl.DeviceIdType.MESH
TRAIN_DEV = 12
VAL_DEV = 4
HOPS = 3
TOK = 64
R = 1024
LAYERS = 8
RING = 16
LAST = 7
COLUMNS = 16
SUMS = 16
UP, DOWN = 0, 1
OWN, OTHER = 0, 1
CHUNKS = [(p, g) for p in range(2) for g in range(2)]
TURNED = {UP: [(8, 0, 1), (8, 1, 0), (8, 1, 1)], DOWN: [(15, 1, 0), (15, 1, 1)]}
TURNS = max(len(TURNED[UP]), len(TURNED[DOWN]), 1)
HEAD = 1
ORDER = {UP: [(OWN, 0), (OTHER, 0), (OTHER, 1), (OWN, 1)], DOWN: [(OWN, 0), (OTHER, 0), (OWN, 1), (OTHER, 1)]}
BOTH = pl.ds(0, 2)


def chip(column, z, core):
    column, z = lax.rem(column + COLUMNS, COLUMNS), lax.rem(z + RING, RING)
    return (column * 2 + z // LAYERS) * 2 + core, lax.rem(z, LAYERS)


def quarter(i):
    return pl.ds(i * TOK, TOK)


def kernel(
    train, val, out, tokens, own, held, last, turned, act_gram, total, parts, load_sem, stage_send, stage_recv, give_send,
    give_recv, send_sem, recv_sem, cross_recv, turned_send, turned_recv, pass_send, pass_recv, sum_send, sum_recv,
):
    blk, layer = lax.axis_index("blk"), lax.axis_index("layer")
    core, column = lax.rem(blk, 2), blk // 4
    z = lax.rem(blk // 2, 2) * LAYERS + layer
    sibling = (blk + 1 - 2 * core, layer)

    def remote(src, dst, sent, received, device):
        return pltpu.make_async_remote_copy(src, dst, sent, received, device_id=device, device_id_type=MESH)

    def target(step, d, on_core):
        if d == UP:
            crosses = ((z == 0) & (step >= 1)) | ((z == 9) & (step == 1))
            return chip(column + crosses.astype(jnp.int32), z + 1, on_core)
        crosses = ((z == 7) & (step >= 1)) | ((z == 14) & (step == 1))
        return chip(column + crosses.astype(jnp.int32), z - 1, on_core)

    barrier = pltpu.get_barrier_semaphore()

    def greet(device):
        pl.semaphore_signal(barrier, inc=1, device_id=device, device_id_type=MESH)

    @pl.when(core == 0)
    def _():
        greet(chip(column, z - 1, 0))
        greet(chip(column, z + 1, 1))

        @pl.when((z == 1) | (z == 10))
        def _():
            greet(chip(column - 1, z - 1, 0))

        @pl.when(z == 6)
        def _():
            greet(chip(column - 1, z + 1, 1))

    @pl.when(core == 1)
    def _():
        greet(chip(column, z + 1, 1))

        @pl.when((z == 6) | (z == 13))
        def _():
            greet(chip(column - 1, z + 1, 1))

    greet(sibling)
    more_up = (core == 0) & ((z == 0) | (z == 9))
    more_down = (core == 1) & ((z == 7) | (z == 14))
    last_down = (core == 1) & (z == 7)
    pl.semaphore_wait(
        barrier,
        2 + core + more_up.astype(jnp.int32) + more_down.astype(jnp.int32) + last_down.astype(jnp.int32),
    )

    def ring(step, d, which, p, g):
        first = isinstance(step, int) and step == 0
        src = val.at[2 * d + p, g] if first and which == OWN else held.at[step, which, p, g]
        sem = 1 if isinstance(g, int) else 0
        on_core, received = d, recv_sem.at[step, which, p, sem]
        if isinstance(step, int) and step == LAST:
            dst = last.at[p, g, quarter((2 if which == d else 0) + d)]
            received = recv_sem.at[step, which, p, g]
            sem = g
            if d == DOWN and which == OTHER:
                on_core, received = 0, cross_recv.at[p, g]
        else:
            dst = held.at[step + 1, which, p, g]
        return remote(src, dst, send_sem.at[step, which, p, sem], received, target(step, d, on_core))

    def starts_at(step, d):
        return lax.rem(z - step + RING, RING) if d == UP else lax.rem(z + step, RING)

    def goes(step, d, which, p, use):
        away = {}
        if which == d:
            for start, turned_p, g in TURNED[1 - d]:
                if turned_p == p:
                    away.setdefault(start, []).append(g)
        if not away:
            use(BOTH)
            return
        start_here = starts_at(step, d)
        whole = start_here >= 0
        for start, gone in away.items():
            whole &= start_here != start
            for g in range(2):
                if g not in gone:
                    pl.when(start_here == start)(lambda: use(g))
        pl.when(whole)(lambda: use(BOTH))

    def ends(step, d, which, p, g, use):
        goes_round = starts_at(step, d) >= 0
        away = [start for start, turned_p, turned_g in TURNED[1 - d] if which == d and (turned_p, turned_g) == (p, g)]
        for start in away:
            goes_round &= starts_at(step, d) != start
        if away:
            pl.when(goes_round)(use)
        else:
            use()

    def turn(i, step, d):
        _, p, g = TURNED[d][i]
        first = isinstance(step, int) and step == 0
        final = isinstance(step, int) and step == LAST
        here = last.at[p, g, quarter(3 if d == UP else 2)]
        if first:
            src = val.at[2 + p, g] if d == UP else here
        else:
            src = turned.at[i]
        return remote(
            src, here if final else turned.at[i], turned_send.at[i], turned_recv.at[i], target(step, d, 0 if final else d)
        )

    def stage(p):
        half = 2 * (1 - core) + p
        return remote(val.at[half], held.at[0, OTHER, p], stage_send.at[p], stage_recv.at[p], sibling)

    def give(p, g, d):
        return remote(
            val.at[2 * d + p, g], last.at[p, g, quarter(2 + d)], give_send.at[p, g, d], give_recv.at[p, g, d], sibling
        )

    def hand_over(d, p, g):
        here = last.at[p, g, quarter(d)]
        return remote(here, here, pass_send.at[p, g], pass_recv.at[p, g], sibling)

    for d in range(2):

        @pl.when(core == d)
        def _():
            for which, p in ORDER[d][:HEAD]:
                goes(0, d, which, p, lambda g: ring(0, d, which, p, g).start())

    for p in range(2):
        stage(p).start()
    loads = [pltpu.make_async_copy(val.at[:, g], own.at[g], load_sem.at[0, g]) for g in range(2)]
    loads += [pltpu.make_async_copy(train.at[:, g], tokens.at[g], load_sem.at[1, g]) for g in range(2)]
    for copy in loads:
        copy.start()

    for d in range(2):

        @pl.when(core == d)
        def _():
            for which, p in ORDER[d][HEAD:]:
                if which == OTHER:
                    stage(p).wait_recv()
                goes(0, d, which, p, lambda g: ring(0, d, which, p, g).start())
            if d == UP:
                for i in range(len(TURNED[UP])):
                    pl.when(z == TURNED[UP][i][0])(lambda: turn(i, 0, UP).start())
                for half in range(2):
                    for p, g in CHUNKS:
                        give(p, g, half).start()
            else:
                for p, g in CHUNKS:
                    give(p, g, 0).wait_recv()
                for i in range(len(TURNED[DOWN])):
                    pl.when(z == TURNED[DOWN][i][0])(lambda: turn(i, 0, DOWN).start())

    total[...] = jnp.zeros_like(total)

    def gram(g, rows):
        return lax.dot_general(
            tokens[g].reshape(TRAIN_DEV * TOK, R),
            rows,
            (((1,), (1,)), ((), ())),
            preferred_element_type=jnp.float32,
        )

    def put_scores(act, grad, rows):
        sums = jnp.sum((act * grad).reshape(TRAIN_DEV, TOK, 4 * TOK), axis=1)
        sums = jnp.concatenate([sums, jnp.zeros((SUMS - TRAIN_DEV, 4 * TOK), jnp.float32)], axis=0)
        sums = jnp.sum(sums.T.reshape(4, TOK, SUMS), axis=1)
        for i, row in enumerate(rows):
            total[pl.ds(row, 1), pl.ds(0, SUMS)] = sums[i : i + 1]

    for copy in loads:
        copy.wait()
    put_scores(*(gram(g, own[g].reshape(4 * TOK, R)) for g in range(2)), range(VAL_DEV))

    for d in range(2):

        @pl.when(core == d)
        def _():
            def step_body(step, carry):
                for which, p in ORDER[d]:

                    def send_on(g):
                        ring(step - 1, d, which, p, g).wait_recv()
                        ring(step, d, which, p, g).start()

                    goes(step, d, which, p, send_on)
                for i in range(len(TURNED[d])):

                    @pl.when(starts_at(step, d) == TURNED[d][i][0])
                    def _():
                        turn(i, step, d).wait_recv()
                        turn(i, step, d).start()

                @pl.when(step >= 3)
                def _():
                    for which, p in ORDER[d]:
                        goes(step - 2, d, which, p, lambda g: ring(step - 2, d, which, p, g).wait_send())

                return carry

            lax.fori_loop(1, LAST, step_body, 0)
            for which, p in ORDER[d]:
                goes(LAST, d, which, p, lambda g: ring(LAST - 1, d, which, p, g).wait_recv())
                for g in range(2):
                    ends(LAST, d, which, p, g, lambda: ring(LAST, d, which, p, g).start())
            for i in range(len(TURNED[d])):

                @pl.when(starts_at(LAST, d) == TURNED[d][i][0])
                def _():
                    turn(i, 1, d).wait_recv()
                    turn(i, LAST, d).start()

    def clear(steps):
        for d in range(2):

            @pl.when(core == d)
            def _():
                for which, p in ORDER[d]:
                    for step in steps:
                        goes(step, d, which, p, lambda g: ring(step, d, which, p, g).wait_send())

    clear((0, LAST - 2))
    for p in range(2):
        stage(p).wait_send()

    @pl.when(core == 0)
    def _():
        for p, g in CHUNKS:
            for half in range(2):
                give(p, g, half).wait_send()

    def pass_on(d, p):
        for g in range(2):
            ring(LAST, d, OTHER if d == UP else OWN, p, g).wait_recv()
            hand_over(d, p, g).start()

    for p in range(2):

        @pl.when((core == 0) & ((z != 0) if p else (z >= 0)))
        def _():
            pass_on(UP, p)

        if p == 0:
            @pl.when((core == 0) & (z == 0))
            def _():
                pass_on(UP, 1)

        @pl.when(core == 1)
        def _():
            pass_on(DOWN, p)

        if p == 1:
            clear((LAST - 1,))

        for g in range(2):

            @pl.when(core == 0)
            def _():
                hand_over(DOWN, p, g).wait_recv()
                for way, which in ((DOWN, OTHER), (UP, OWN)):
                    straight = z >= 0
                    for i, (start, turned_p, turned_g) in enumerate(TURNED[1 - way]):
                        if (turned_p, turned_g) == (p, g):
                            here = z == (start + LAYERS) % RING
                            straight &= jnp.logical_not(here)
                            pl.when(here)(lambda: turn(i, LAST, 1 - way).wait_recv())
                    pl.when(straight)(lambda: ring(LAST, way, which, p, g).wait_recv())

            @pl.when(core == 1)
            def _():
                hand_over(UP, p, g).wait_recv()
                give(p, g, 1).wait_recv()

            if g == 0:
                act_gram[...] = gram(g, last[p, g])
            else:
                one, two = (1 + core) * VAL_DEV + p, (2 - core) * VAL_DEV + p
                put_scores(act_gram[...], gram(g, last[p, g]), (one, one + 2, two, two + 2))

    parts[layer] = total[...]

    def share(peer, sender):
        return remote(total, parts.at[sender], sum_send.at[peer], sum_recv.at[sender], (blk, peer))

    for peer in range(LAYERS):

        @pl.when(peer != layer)
        def _():
            share(peer, layer).start()

    for d in range(2):

        @pl.when(core == d)
        def _():
            for which, p in ORDER[d]:
                for g in range(2):
                    ends(LAST, d, which, p, g, lambda: ring(LAST, d, which, p, g).wait_send())
            for p, g in CHUNKS:
                hand_over(d, p, g).wait_send()
            for i in range(len(TURNED[d])):
                past = z - TURNED[d][i][0] if d == UP else TURNED[d][i][0] - z
                pl.when(lax.rem(past + RING, RING) <= LAST)(lambda: turn(i, 0, d).wait_send())


    for peer in range(LAYERS):

        @pl.when(peer != layer)
        def _():
            share(peer, peer).wait_recv()
            share(peer, layer).wait_send()

    out[...] = jnp.sum(parts[...], axis=0)


def local(train_factors, val_factors):
    train = train_factors.reshape(TRAIN_DEV, 2, TOK, R)
    val = val_factors.reshape(VAL_DEV, 2, TOK, R)
    dma = pltpu.SemaphoreType.DMA
    summed = pl.pallas_call(
        kernel,
        out_shape=jax.ShapeDtypeStruct((SUMS, 128), jnp.float32),
        in_specs=[pl.BlockSpec(memory_space=pl.ANY)] * 2,
        out_specs=pl.BlockSpec(memory_space=pltpu.VMEM),
        scratch_shapes=[
            pltpu.VMEM((2, TRAIN_DEV, TOK, R), jnp.bfloat16),
            pltpu.VMEM((2, VAL_DEV, TOK, R), jnp.bfloat16),
            pltpu.VMEM((LAST + 1, 2, 2, 2, TOK, R), jnp.bfloat16),
            pltpu.VMEM((2, 2, 4 * TOK, R), jnp.bfloat16),
            pltpu.VMEM((TURNS, TOK, R), jnp.bfloat16),
            pltpu.VMEM((TRAIN_DEV * TOK, 4 * TOK), jnp.float32),
            pltpu.VMEM((SUMS, 128), jnp.float32),
            pltpu.VMEM((LAYERS, SUMS, 128), jnp.float32),
            dma((2, 2)),
            dma((2,)),
            dma((2,)),
            dma((2, 2, 2)),
            dma((2, 2, 2)),
            dma((LAST + 1, 2, 2, 2)),
            dma((LAST + 1, 2, 2, 2)),
            dma((2, 2)),
            dma((TURNS,)),
            dma((TURNS,)),
            dma((2, 2)),
            dma((2, 2)),
            dma((LAYERS,)),
            dma((LAYERS,)),
        ],
        compiler_params=pltpu.CompilerParams(
            collective_id=0, has_side_effects=True, vmem_limit_bytes=53 * 2**20
        ),
        name="score_ring",
    )(train, val)
    scores = summed[: HOPS * VAL_DEV, :TRAIN_DEV]
    return scores.reshape(HOPS, VAL_DEV, TRAIN_DEV).transpose(2, 0, 1)


def solution(mesh):
    return jax.shard_map(
        local,
        mesh=mesh,
        in_specs=(P("blk", "layer", None, None, None), P("blk", "layer", None, None, None)),
        out_specs=P("blk", None, None),
        check_vma=False,
    )
```

```python
import jax
import jax.numpy as jnp
from jax import lax
from jax.experimental import pallas as pl
from jax.experimental.pallas import tpu as pltpu
from jax.sharding import PartitionSpec as P

MESH = pl.DeviceIdType.MESH
TRAIN_DEV = 12
VAL_DEV = 4
HOPS = 3
TOK = 64
R = 1024
LAYERS = 8
RING = 16
LAST = 7
COLUMNS = 16
SUMS = 16
UP, DOWN = 0, 1
OWN, OTHER = 0, 1
CHUNKS = [(p, g) for p in range(2) for g in range(2)]
TURNED = {UP: [(8, 0, 1), (8, 1, 0), (8, 1, 1)], DOWN: [(15, 1, 0), (15, 1, 1)]}
TURNS = max(len(TURNED[UP]), len(TURNED[DOWN]), 1)
HEAD = 1
ORDER = {UP: [(OWN, 0), (OTHER, 0), (OTHER, 1), (OWN, 1)], DOWN: [(OWN, 0), (OTHER, 0), (OWN, 1), (OTHER, 1)]}
BOTH = pl.ds(0, 2)


def chip(column, z, core):
    column, z = lax.rem(column + COLUMNS, COLUMNS), lax.rem(z + RING, RING)
    return (column * 2 + z // LAYERS) * 2 + core, lax.rem(z, LAYERS)


def quarter(i):
    return pl.ds(i * TOK, TOK)


def kernel(
    train, val, out, tokens, own, held, last, turned, act_gram, total, parts, load_sem, stage_send, stage_recv, give_send,
    give_recv, send_sem, recv_sem, cross_recv, turned_send, turned_recv, pass_send, pass_recv, sum_send, sum_recv,
):
    blk, layer = lax.axis_index("blk"), lax.axis_index("layer")
    core, column = lax.rem(blk, 2), blk // 4
    z = lax.rem(blk // 2, 2) * LAYERS + layer
    sibling = (blk + 1 - 2 * core, layer)

    def remote(src, dst, sent, received, device):
        return pltpu.make_async_remote_copy(src, dst, sent, received, device_id=device, device_id_type=MESH)

    def target(step, d, on_core):
        if d == UP:
            crosses = ((z == 0) & (step >= 1)) | ((z == 9) & (step == 1))
            return chip(column + crosses.astype(jnp.int32), z + 1, on_core)
        crosses = ((z == 7) & (step >= 1)) | ((z == 14) & (step == 1))
        return chip(column + crosses.astype(jnp.int32), z - 1, on_core)

    barrier = pltpu.get_barrier_semaphore()

    def greet(device):
        pl.semaphore_signal(barrier, inc=1, device_id=device, device_id_type=MESH)

    @pl.when(core == 0)
    def _():
        greet(chip(column, z - 1, 0))
        greet(chip(column, z + 1, 1))

        @pl.when((z == 1) | (z == 10))
        def _():
            greet(chip(column - 1, z - 1, 0))

        @pl.when(z == 6)
        def _():
            greet(chip(column - 1, z + 1, 1))

    @pl.when(core == 1)
    def _():
        greet(chip(column, z + 1, 1))

        @pl.when((z == 6) | (z == 13))
        def _():
            greet(chip(column - 1, z + 1, 1))

    greet(sibling)
    more_up = (core == 0) & ((z == 0) | (z == 9))
    more_down = (core == 1) & ((z == 7) | (z == 14))
    last_down = (core == 1) & (z == 7)
    pl.semaphore_wait(
        barrier,
        2 + core + more_up.astype(jnp.int32) + more_down.astype(jnp.int32) + last_down.astype(jnp.int32),
    )

    def ring(step, d, which, p, g):
        first = isinstance(step, int) and step == 0
        src = val.at[2 * d + p, g] if first and which == OWN else held.at[step, which, p, g]
        sem = 1 if isinstance(g, int) else 0
        on_core, received = d, recv_sem.at[step, which, p, sem]
        if isinstance(step, int) and step == LAST:
            dst = last.at[p, g, quarter((2 if which == d else 0) + d)]
            received = recv_sem.at[step, which, p, g]
            sem = g
            if d == DOWN and which == OTHER:
                on_core, received = 0, cross_recv.at[p, g]
        else:
            dst = held.at[step + 1, which, p, g]
        return remote(src, dst, send_sem.at[step, which, p, sem], received, target(step, d, on_core))

    def starts_at(step, d):
        return lax.rem(z - step + RING, RING) if d == UP else lax.rem(z + step, RING)

    def goes(step, d, which, p, use):
        away = {}
        if which == d:
            for start, turned_p, g in TURNED[1 - d]:
                if turned_p == p:
                    away.setdefault(start, []).append(g)
        if not away:
            use(BOTH)
            return
        start_here = starts_at(step, d)
        whole = start_here >= 0
        for start, gone in away.items():
            whole &= start_here != start
            for g in range(2):
                if g not in gone:
                    pl.when(start_here == start)(lambda: use(g))
        pl.when(whole)(lambda: use(BOTH))

    def ends(step, d, which, p, g, use):
        goes_round = starts_at(step, d) >= 0
        away = [start for start, turned_p, turned_g in TURNED[1 - d] if which == d and (turned_p, turned_g) == (p, g)]
        for start in away:
            goes_round &= starts_at(step, d) != start
        if away:
            pl.when(goes_round)(use)
        else:
            use()

    def turn(i, step, d):
        _, p, g = TURNED[d][i]
        first = isinstance(step, int) and step == 0
        final = isinstance(step, int) and step == LAST
        here = last.at[p, g, quarter(3 if d == UP else 2)]
        if first:
            src = val.at[2 + p, g] if d == UP else here
        else:
            src = turned.at[i]
        return remote(
            src, here if final else turned.at[i], turned_send.at[i], turned_recv.at[i], target(step, d, 0 if final else d)
        )

    def stage(p):
        half = 2 * (1 - core) + p
        return remote(val.at[half], held.at[0, OTHER, p], stage_send.at[p], stage_recv.at[p], sibling)

    def give(p, g, d):
        return remote(
            val.at[2 * d + p, g], last.at[p, g, quarter(2 + d)], give_send.at[p, g, d], give_recv.at[p, g, d], sibling
        )

    def hand_over(d, p, g):
        here = last.at[p, g, quarter(d)]
        return remote(here, here, pass_send.at[p, g], pass_recv.at[p, g], sibling)

    for d in range(2):

        @pl.when(core == d)
        def _():
            for which, p in ORDER[d][:HEAD]:
                goes(0, d, which, p, lambda g: ring(0, d, which, p, g).start())

    for p in range(2):
        stage(p).start()
    loads = [pltpu.make_async_copy(val.at[:, g], own.at[g], load_sem.at[0, g]) for g in range(2)]
    loads += [pltpu.make_async_copy(train.at[:, g], tokens.at[g], load_sem.at[1, g]) for g in range(2)]
    for copy in loads:
        copy.start()

    for d in range(2):

        @pl.when(core == d)
        def _():
            for which, p in ORDER[d][HEAD:]:
                if which == OTHER:
                    stage(p).wait_recv()
                goes(0, d, which, p, lambda g: ring(0, d, which, p, g).start())
            if d == UP:
                for i in range(len(TURNED[UP])):
                    pl.when(z == TURNED[UP][i][0])(lambda: turn(i, 0, UP).start())
                for half in range(2):
                    for p, g in CHUNKS:
                        give(p, g, half).start()
            else:
                for p, g in CHUNKS:
                    give(p, g, 0).wait_recv()
                for i in range(len(TURNED[DOWN])):
                    pl.when(z == TURNED[DOWN][i][0])(lambda: turn(i, 0, DOWN).start())

    total[...] = jnp.zeros_like(total)

    def gram(g, rows):
        return lax.dot_general(
            tokens[g].reshape(TRAIN_DEV * TOK, R),
            rows,
            (((1,), (1,)), ((), ())),
            preferred_element_type=jnp.float32,
        )

    def put_scores(act, grad, rows):
        sums = jnp.sum((act * grad).reshape(TRAIN_DEV, TOK, 4 * TOK), axis=1)
        sums = jnp.concatenate([sums, jnp.zeros((SUMS - TRAIN_DEV, 4 * TOK), jnp.float32)], axis=0)
        sums = jnp.sum(sums.T.reshape(4, TOK, SUMS), axis=1)
        for i, row in enumerate(rows):
            total[pl.ds(row, 1), pl.ds(0, SUMS)] = sums[i : i + 1]

    for copy in loads:
        copy.wait()
    put_scores(*(gram(g, own[g].reshape(4 * TOK, R)) for g in range(2)), range(VAL_DEV))

    for d in range(2):

        @pl.when(core == d)
        def _():
            def step_body(step, carry):
                for which, p in ORDER[d]:

                    def send_on(g):
                        ring(step - 1, d, which, p, g).wait_recv()
                        ring(step, d, which, p, g).start()

                    goes(step, d, which, p, send_on)
                for i in range(len(TURNED[d])):

                    @pl.when(starts_at(step, d) == TURNED[d][i][0])
                    def _():
                        turn(i, step, d).wait_recv()
                        turn(i, step, d).start()

                @pl.when(step >= 3)
                def _():
                    for which, p in ORDER[d]:
                        goes(step - 2, d, which, p, lambda g: ring(step - 2, d, which, p, g).wait_send())

                return carry

            lax.fori_loop(1, LAST, step_body, 0)
            for which, p in ORDER[d]:
                goes(LAST, d, which, p, lambda g: ring(LAST - 1, d, which, p, g).wait_recv())
                for g in range(2):
                    ends(LAST, d, which, p, g, lambda: ring(LAST, d, which, p, g).start())
            for i in range(len(TURNED[d])):

                @pl.when(starts_at(LAST, d) == TURNED[d][i][0])
                def _():
                    turn(i, 1, d).wait_recv()
                    turn(i, LAST, d).start()

    def clear(steps):
        for d in range(2):

            @pl.when(core == d)
            def _():
                for which, p in ORDER[d]:
                    for step in steps:
                        goes(step, d, which, p, lambda g: ring(step, d, which, p, g).wait_send())

    clear((0, LAST - 2))
    for p in range(2):
        stage(p).wait_send()

    @pl.when(core == 0)
    def _():
        for p, g in CHUNKS:
            for half in range(2):
                give(p, g, half).wait_send()

    def pass_on(d, p):
        for g in range(2):
            ring(LAST, d, OTHER if d == UP else OWN, p, g).wait_recv()
            hand_over(d, p, g).start()

    for p in range(2):

        @pl.when((core == 0) & ((z != 0) if p else (z >= 0)))
        def _():
            pass_on(UP, p)

        if p == 0:
            @pl.when((core == 0) & (z == 0))
            def _():
                pass_on(UP, 1)

        @pl.when(core == 1)
        def _():
            pass_on(DOWN, p)

        if p == 1:
            clear((LAST - 1,))

        for g in range(2):

            @pl.when(core == 0)
            def _():
                hand_over(DOWN, p, g).wait_recv()
                for way, which in ((DOWN, OTHER), (UP, OWN)):
                    straight = z >= 0
                    for i, (start, turned_p, turned_g) in enumerate(TURNED[1 - way]):
                        if (turned_p, turned_g) == (p, g):
                            here = z == (start + LAYERS) % RING
                            straight &= jnp.logical_not(here)
                            pl.when(here)(lambda: turn(i, LAST, 1 - way).wait_recv())
                    pl.when(straight)(lambda: ring(LAST, way, which, p, g).wait_recv())

            @pl.when(core == 1)
            def _():
                hand_over(UP, p, g).wait_recv()
                give(p, g, 1).wait_recv()

            if g == 0:
                act_gram[...] = gram(g, last[p, g])
            else:
                one, two = (1 + core) * VAL_DEV + p, (2 - core) * VAL_DEV + p
                put_scores(act_gram[...], gram(g, last[p, g]), (one, one + 2, two, two + 2))

    parts[layer] = total[...]

    def share(peer, sender):
        return remote(total, parts.at[sender], sum_send.at[peer], sum_recv.at[sender], (blk, peer))

    for peer in range(LAYERS):

        @pl.when(peer != layer)
        def _():
            share(peer, layer).start()

    for d in range(2):

        @pl.when(core == d)
        def _():
            for which, p in ORDER[d]:
                for g in range(2):
                    ends(LAST, d, which, p, g, lambda: ring(LAST, d, which, p, g).wait_send())
            for p, g in CHUNKS:
                hand_over(d, p, g).wait_send()
            for i in range(len(TURNED[d])):
                past = z - TURNED[d][i][0] if d == UP else TURNED[d][i][0] - z
                pl.when(lax.rem(past + RING, RING) <= LAST)(lambda: turn(i, 0, d).wait_send())


    for peer in range(LAYERS):

        @pl.when(peer != layer)
        def _():
            share(peer, peer).wait_recv()
            share(peer, layer).wait_send()

    sums = jnp.sum(parts[...], axis=0)
    for hop in range(HOPS):
        out[hop] = sums[hop * VAL_DEV : (hop + 1) * VAL_DEV, :TRAIN_DEV]


def local(train_factors, val_factors):
    train = train_factors.reshape(TRAIN_DEV, 2, TOK, R)
    val = val_factors.reshape(VAL_DEV, 2, TOK, R)
    dma = pltpu.SemaphoreType.DMA
    summed = pl.pallas_call(
        kernel,
        out_shape=jax.ShapeDtypeStruct((HOPS, VAL_DEV, TRAIN_DEV), jnp.float32),
        in_specs=[pl.BlockSpec(memory_space=pl.ANY)] * 2,
        out_specs=pl.BlockSpec(memory_space=pltpu.VMEM),
        scratch_shapes=[
            pltpu.VMEM((2, TRAIN_DEV, TOK, R), jnp.bfloat16),
            pltpu.VMEM((2, VAL_DEV, TOK, R), jnp.bfloat16),
            pltpu.VMEM((LAST + 1, 2, 2, 2, TOK, R), jnp.bfloat16),
            pltpu.VMEM((2, 2, 4 * TOK, R), jnp.bfloat16),
            pltpu.VMEM((TURNS, TOK, R), jnp.bfloat16),
            pltpu.VMEM((TRAIN_DEV * TOK, 4 * TOK), jnp.float32),
            pltpu.VMEM((SUMS, 128), jnp.float32),
            pltpu.VMEM((LAYERS, SUMS, 128), jnp.float32),
            dma((2, 2)),
            dma((2,)),
            dma((2,)),
            dma((2, 2, 2)),
            dma((2, 2, 2)),
            dma((LAST + 1, 2, 2, 2)),
            dma((LAST + 1, 2, 2, 2)),
            dma((2, 2)),
            dma((TURNS,)),
            dma((TURNS,)),
            dma((2, 2)),
            dma((2, 2)),
            dma((LAYERS,)),
            dma((LAYERS,)),
        ],
        compiler_params=pltpu.CompilerParams(
            collective_id=0, has_side_effects=True, vmem_limit_bytes=53 * 2**20
        ),
        name="score_ring",
    )(train, val)

    return summed.transpose(2, 0, 1)


def solution(mesh):
    return jax.shard_map(
        local,
        mesh=mesh,
        in_specs=(P("blk", "layer", None, None, None), P("blk", "layer", None, None, None)),
        out_specs=P("blk", None, None),
        check_vma=False,
    )
```
